32 devices in a mesh: req: 4 (over z), head: 2 (over core), grp: 4 (over y, x).
Axes of the slice: x: 2, y: 2, z: 4, core: 2. Of those that a mesh axis runs over, the one named last changes fastest.
Arguments:
- residual: bfloat16 [128, 7168], P(('req', 'grp'), 'head'), may hold values from -12 to 12
- attn_part: bfloat16 [2, 128, 7168], P('head', ('req', 'grp')), may hold values from -6 to 6
- norm_gain: float32 [7168], P('head'), may hold values from 0.1 to 1.9
- routes: int32 [128, 8], P(('req', 'grp')), may hold values from 0 to 31, all different within a row; in each aligned block of 8 rows (0 to 7, 8 to 15, ...) at most 4 rows name the same one
- gates: float32 [128, 8], P(('req', 'grp')), may hold values from 0.1 to 0.6
- gate_weight: bfloat16 [32, 7168, 2048], P('req', None, ('head', 'grp')), may hold values from -0.0625 to 0.0625
- up_weight: bfloat16 [32, 7168, 2048], P('req', None, ('head', 'grp')), may hold values from -0.0625 to 0.0625
- down_weight: bfloat16 [32, 2048, 7168], P('req', None, ('head', 'grp')), may hold values from -0.125 to 0.125
Outputs:
- mixed: bfloat16 [128, 7168], P(('req', 'grp'), 'head')
The draws below stay inside these ranges and needn't reach their ends.
Inputs may be any that keep to these rules, and one draw needn't show every extreme that they name: `routes`: each row names 8 different experts. In each aligned block of 8 rows (the rows of one index pair of req and grp) no expert is named more than 4 times, a bound that some block reaches.
All inputs are finite; a program needn't handle non-finite values.
Results may differ from the reference program's by a relative error of at most 0.012.
Values may be sent and summed in bfloat16 or wider, within the bound.
No kernel may reach another device: no remote copies, remote signals or barrier semaphores. Data moves between devices by JAX's collectives and lax.ppermute only.
A program may use at most 192 MiB of HBM per device.

```python
import math
import jax
import jax.numpy as jnp
import numpy as np
from jax import lax

D = 7168
FF = 2048
TOP = 8
EXPERTS = 32
TOK_DEV = 8
CAP = 4
TOKENS = 128


def draw_residual(key, part):
    key = jax.random.fold_in(key, 11)
    columns = jnp.arange(D)
    values = jax.random.normal(key, (TOKENS, D), jnp.float32)
    scale = jnp.where(columns < D // 2, 0.4, 2.0)
    return jnp.clip(values * scale[None, :], -12.0, 12.0).astype(jnp.bfloat16)


def with_spikes(drawn, own_key, source, target, blocks, factor):
    owner, partner = [(jnp.arange(drawn.shape[dim]) // (drawn.shape[dim] // blocks)).reshape([-1 if axis == dim else 1 for axis in range(drawn.ndim)]) for dim in (source, target)]
    chosen = jax.random.permutation(own_key, blocks)[partner]
    strong = (owner == chosen) | (owner == (partner + blocks // 2) % blocks)
    return jnp.where(strong, factor * drawn, drawn)


def levels(stream_key, dims, shards, low, top_value):
    def one(dim, blocks):
        heights = jax.random.uniform(jax.random.fold_in(jax.random.fold_in(stream_key, 6), dim), (blocks,), jnp.float32, low / len(shards), top_value / len(shards))
        return jnp.repeat(jnp.exp(heights), dims[dim] // blocks).reshape((-1,) + (1,) * (len(dims) - dim - 1))

    level = one(*shards[0])
    for cut in shards[1:]:
        level = level * one(*cut)
    return level


def deal_out(rng, own, number, rows, count, top, bound, lean):
    ranking = jax.random.permutation(rng, count)
    crowded, usual = shares(count, rows * top, bound, lean, True), shares(count, rows * top, bound, lean, False)
    places = jnp.arange(count)

    def named(tallies, turn):
        used = int((tallies > 0).sum())
        fixed = max(1, used // 4)
        moved = fixed + (places - fixed + turn * (used - fixed)) % max(1, count - fixed)
        return jnp.zeros((count,), jnp.int32).at[ranking[jnp.where(places < fixed, places, moved)]].set(jnp.asarray(tallies, jnp.int32))

    tallies = jnp.where(number % 4 == 0, named(crowded, number // 4), named(usual, number - number // 4 - 1))
    mixed = jax.random.permutation(jax.random.fold_in(own, 3), count)
    donor, sink = mixed[0:count // 2 * 2:2], mixed[1:count // 2 * 2:2]
    margin = jnp.minimum(tallies[donor] - 1, bound - tallies[sink]) // 2
    margin = jnp.where((donor == ranking[0]) | (sink == ranking[0]) | (tallies[sink] == 0), 0, jnp.maximum(margin, 0))
    moved = jax.random.randint(jax.random.fold_in(own, 4), (count // 2,), 0, 1 << 20) % (margin + 1)
    tallies = tallies.at[donor].add(-moved).at[sink].add(moved)
    items = jnp.searchsorted(jnp.cumsum(tallies), jnp.arange(rows * top), side="right").astype(jnp.int32)
    table = items.reshape(top, rows).T
    table = table[jax.random.permutation(jax.random.fold_in(own, 1), rows)]
    turn = jax.random.randint(jax.random.fold_in(own, 2), (rows, 1), 0, top)
    return jnp.take_along_axis(table, (jnp.arange(top)[None, :] + turn) % top, axis=1)


def shares(amount, total, reach, slope, full):
    loads = [(1 << 20) // math.isqrt(standing ** slope) + 1 for standing in range(1, amount + 1)]
    largest = reach if full else min(reach, max(-(-total // amount), total * loads[0] // sum(loads)))
    least = 1 if total - largest >= amount - 1 else 0
    counts, rest = [largest] + [least] * (amount - 1), total - largest - least * (amount - 1)
    while rest > 0:
        movable = [i for i in range(1, amount) if counts[i] < largest] or [i for i in range(1, amount) if counts[i] < reach]
        pool, left = sum([loads[i] for i in movable]), rest
        for i in movable:
            more = min(reach - counts[i], max(1, left * loads[i] // pool), rest)
            counts[i] = counts[i] + more
            rest = rest - more
    return np.array(counts)


def normal_values(key, shape, scale, reach, cuts=(), held_as=jnp.bfloat16):
    gain = levels(key, shape, cuts, -0.22, 0.18) if cuts else 1.0
    drawn = jax.random.normal(key, shape, jnp.float32) * scale * gain
    return jnp.minimum(jnp.maximum(drawn, -reach), reach).astype(held_as)


def heavy_noise(own_key, dims, deviation, limit, cuts, heavy, kind=jnp.bfloat16):
    drawn = deviation * jax.random.normal(own_key, dims, jnp.float32)
    if cuts:
        drawn = drawn * levels(own_key, dims, cuts, -0.22, 0.18)
    return jnp.clip(with_spikes(drawn, jax.random.fold_in(own_key, 3), *heavy), -limit, limit).astype(kind)


def setup_inputs(seed: int = 0) -> dict:
    keys = jax.random.split(jax.random.key(seed), 9)
    residual = draw_residual(jax.random.fold_in(keys[8], 71), 0)
    attn_part = heavy_noise(keys[1], (2, TOKENS, D), 0.7, 6.0, ((0, 2), (1, 16)), (0, 2, 2, 2.0))
    norm_gain = jnp.clip(1.0 + 0.18 * jax.random.normal(keys[2], (D,), jnp.float32), 0.1, 1.9)
    routes_keys = jax.random.split(jax.random.fold_in(keys[3], 1), TOKENS // TOK_DEV)
    routes_turns = jax.random.permutation(jax.random.fold_in(keys[3], 3), TOKENS // TOK_DEV)
    routes = jax.vmap(lambda own, number: deal_out(jax.random.fold_in(keys[3], 2), own, number, TOK_DEV, EXPERTS, TOP, CAP, 2))(routes_keys, routes_turns).reshape((TOKENS, TOP))
    gates = jnp.clip(0.1 + 0.5 * jax.random.uniform(keys[4], (TOKENS, TOP), jnp.float32) ** levels(keys[4], (TOKENS, TOP), ((0, 16),), -0.2, 0.2), 0.1, 0.6)
    gate_weight = normal_values(keys[5], (EXPERTS, D, FF), D ** -0.5, 0.0625, ((0, 4), (2, 8)))
    up_weight = normal_values(keys[6], (EXPERTS, D, FF), D ** -0.5, 0.0625, ((0, 4), (2, 8)))
    down_weight = normal_values(keys[7], (EXPERTS, FF, D), FF ** -0.5, 0.125, ((0, 4), (2, 8)))
    return dict(residual=residual, attn_part=attn_part, norm_gain=norm_gain, routes=routes, gates=gates, gate_weight=gate_weight, up_weight=up_weight, down_weight=down_weight)


EPSILON = 1e-06

def expert_apply(operands):
    rows_in, weight_gate, weight_up, weight_down = operands
    gate_act = jnp.dot(rows_in, weight_gate, preferred_element_type=jnp.float32)
    up_act = jnp.dot(rows_in, weight_up, preferred_element_type=jnp.float32)
    hidden_units = (jax.nn.silu(gate_act) * up_act).astype(jnp.bfloat16)
    return jnp.dot(hidden_units, weight_down, preferred_element_type=jnp.float32).astype(jnp.bfloat16)

def reference(residual, attn_part, norm_gain, routes, gates, gate_weight, up_weight, down_weight):
    attention = attn_part[0].astype(jnp.float32) + attn_part[1].astype(jnp.float32)
    hidden_state = residual.astype(jnp.float32) + attention
    row_scale = lax.rsqrt(lax.optimization_barrier(jnp.mean(hidden_state * hidden_state, axis=1, keepdims=True)) + EPSILON)
    normed = (hidden_state * row_scale * norm_gain[None, :]).astype(jnp.bfloat16)
    blocks = TOKENS // TOK_DEV
    flat_routes = routes.reshape(blocks, TOK_DEV * TOP)
    onehot = (flat_routes[:, :, None] == jnp.arange(EXPERTS, dtype=jnp.int32)[None, None, :]).astype(jnp.int32)
    earlier = jnp.cumsum(onehot, axis=1) - onehot
    slot_index = lax.optimization_barrier(jnp.sum(earlier * onehot, axis=2)).reshape(TOKENS, TOP).astype(jnp.int32)
    block_index = (jnp.arange(TOKENS, dtype=jnp.int32) // TOK_DEV)[:, None]
    position = (block_index * CAP + slot_index).astype(jnp.int32)
    spread_rows = jnp.broadcast_to(normed[:, None, :], (TOKENS, TOP, D))
    buffer = jnp.zeros((EXPERTS, blocks * CAP, D), jnp.bfloat16).at[routes, position].set(spread_rows)
    outputs = lax.map(expert_apply, (buffer, gate_weight, up_weight, down_weight))
    picked = outputs[routes, position].astype(jnp.float32)
    routed = lax.optimization_barrier(jnp.sum(gates[:, :, None] * picked, axis=1))
    return (hidden_state + routed).astype(jnp.bfloat16)
```

```python
import jax
import jax.numpy as jnp
from jax import lax
from jax.experimental import pallas as pl
from jax.experimental.pallas import tpu as pltpu
from jax.sharding import PartitionSpec as P

CAP = 4
EPSILON = 1e-06
TAIL = 128
CUTS = 7
FLIGHT = 4
RING = 3
MIB = 1024 * 1024
VMEM = pl.BlockSpec(memory_space=pltpu.VMEM)
SMEM = pl.BlockSpec(memory_space=pltpu.SMEM)
ANY = pl.BlockSpec(memory_space=pl.ANY)
HBM = pl.BlockSpec(memory_space=pltpu.HBM)


def swap(array, axis, bits):
    return lax.ppermute(array, axis, [(i, i ^ bits) for i in range(lax.axis_size(axis))])


def gather_rows(array, axis, meanwhile):
    count = lax.axis_size(axis)
    if count > 4:
        return lax.all_gather(array, axis, axis=0, tiled=True), meanwhile
    pieces = [array] + [swap(array, axis, bits) for bits in range(1, count)]
    pieces, meanwhile = lax.optimization_barrier((pieces, meanwhile))

    def kernel(*refs):
        refs[-1][...] = jnp.concatenate([ref[...] for ref in refs[:-1]], axis=0)

    rows = pl.pallas_call(
        kernel,
        out_shape=jax.ShapeDtypeStruct((count * array.shape[0], array.shape[1]), array.dtype),
        in_specs=[VMEM] * count,
        out_specs=VMEM,
        compiler_params=pltpu.CompilerParams(vmem_limit_bytes=4 * MIB),
        name="collect",
    )(*pieces)
    return rows, meanwhile


def prepare_kernel(where_ref, *refs):
    sources, (base_ref, tail_ref, out_gain_ref), refs = refs[:5], refs[5:8], refs[8:]
    copies_to, wide_ref, sems = refs[:4], refs[4], refs[5]
    copies = [
        pltpu.make_async_copy(source, target, sems.at[index])
        for index, (source, target) in enumerate(zip(sources, (*copies_to, out_gain_ref)))
    ]
    for copy in copies:
        copy.start()
    for copy in copies:
        copy.wait()
    attn_ref, res_ref, routes_ref, gates_ref = copies_to
    half = res_ref.shape[1]
    top = routes_ref.shape[1]
    here = pl.ds(pl.multiple_of(where_ref[0] * half, 128), half)
    base_ref[...] = attn_ref[...].astype(jnp.float32)
    base_ref[:, here] += res_ref[...].astype(jnp.float32)
    gates = gates_ref[...]
    upper = gates.astype(jnp.bfloat16).astype(jnp.float32)
    middle = (gates - upper).astype(jnp.bfloat16).astype(jnp.float32)
    wide_ref[...] = jnp.zeros_like(wide_ref)
    for index, part in enumerate((routes_ref[...].astype(jnp.float32), upper, middle, gates - upper - middle)):
        wide_ref[:, index * top : (index + 1) * top] = part
    tail_ref[...] = wide_ref[...].astype(jnp.bfloat16)


def prepare(where, attn, residual, routes, gates, gain):
    rows = residual.shape[0]
    arrays = [attn, residual, routes, gates]
    return pl.pallas_call(
        prepare_kernel,
        out_shape=(
            jax.ShapeDtypeStruct(attn.shape, jnp.float32),
            jax.ShapeDtypeStruct((rows, TAIL), jnp.bfloat16),
            jax.ShapeDtypeStruct(gain.shape, jnp.float32),
        ),
        in_specs=[SMEM] + [HBM] * 5,
        out_specs=(VMEM, VMEM, VMEM),
        scratch_shapes=[pltpu.VMEM(array.shape, array.dtype) for array in arrays]
        + [pltpu.VMEM((rows, TAIL), jnp.float32), pltpu.SemaphoreType.DMA((5,))],
        compiler_params=pltpu.CompilerParams(vmem_limit_bytes=4 * MIB),
        name="prepare",
    )(where, *[in_hbm(array) for array in (*arrays, gain)])


def norm_kernel(where_ref, base_ref, attn_there_ref, res_there_ref, gain_ref, tail_ref, hidden_ref, packet_ref):
    half = res_there_ref.shape[1]
    here = pl.ds(pl.multiple_of(where_ref[0] * half, 128), half)
    there = pl.ds(pl.multiple_of((1 - where_ref[0]) * half, 128), half)
    hidden = base_ref[:, here] + attn_there_ref[:, here].astype(jnp.float32)
    other = base_ref[:, there] + attn_there_ref[:, there].astype(jnp.float32) + res_there_ref[...].astype(jnp.float32)
    squares = jnp.sum(hidden * hidden, axis=1, keepdims=True) + jnp.sum(other * other, axis=1, keepdims=True)
    row_scale = lax.rsqrt(squares / (2 * half) + EPSILON)
    hidden_ref[...] = hidden
    packet_ref[:, :half] = (hidden * row_scale * gain_ref[...]).astype(jnp.bfloat16)
    packet_ref[:, half:] = tail_ref[...]


def norm(where, base, attn_there, residual_there, gain, tail):
    rows, half = residual_there.shape
    return pl.pallas_call(
        norm_kernel,
        out_shape=(
            jax.ShapeDtypeStruct((rows, half), jnp.float32),
            jax.ShapeDtypeStruct((rows, half + TAIL), jnp.bfloat16),
        ),
        in_specs=[SMEM] + [VMEM] * 5,
        out_specs=(VMEM, VMEM),
        compiler_params=pltpu.CompilerParams(vmem_limit_bytes=4 * MIB),
        name="norm",
    )(where, base, attn_there, residual_there, gain, tail)


def in_hbm(array):
    return pltpu.with_memory_space_constraint(array, pltpu.HBM)


def in_vmem(array):
    return pltpu.with_memory_space_constraint(array, pltpu.VMEM)


def stage(weights, after=None):
    weights = [(array, first, end) for array, first, end in weights if end > first]
    if not weights:
        return []
    spans = [(first, end) for _, first, end in weights]
    extra = [] if after is None else [after]

    def kernel(*refs):
        inputs, outs, sems = refs[: len(spans)], refs[len(spans) + len(extra) : -1], refs[-1]
        copies = []
        for source, target, (first, end) in zip(inputs, outs, spans):
            for e in range(end - first):
                copies.append(pltpu.make_async_copy(source.at[first + e], target.at[e], sems.at[len(copies)]))
        for copy in copies:
            copy.start()
        for copy in copies:
            copy.wait()

    count = sum(end - first for first, end in spans)
    nbytes = sum((end - first) * array[0].size * 2 for array, first, end in weights)
    copies = pl.pallas_call(
        kernel,
        out_shape=[pltpu.VMEM((end - first, *array.shape[1:]), array.dtype) for array, first, end in weights],
        in_specs=[HBM] * len(spans) + [ANY] * len(extra),
        out_specs=[VMEM] * len(spans),
        scratch_shapes=[pltpu.SemaphoreType.DMA((count,))],
        compiler_params=pltpu.CompilerParams(vmem_limit_bytes=MIB),
        cost_estimate=pl.CostEstimate(flops=0, bytes_accessed=nbytes, transcendentals=0),
        name="stage",
    )(*[in_hbm(array) for array, _, _ in weights], *extra)
    return list(copies)


def shift_of(count):
    return count.bit_length() - 1


def canonical(position, where_ref, sizes):
    reqs, groups, rows = sizes
    req = (position >> shift_of(rows)) & (reqs - 1)
    if reqs <= 4:
        req = req ^ where_ref[1]
    group = (position >> shift_of(rows * reqs)) ^ where_ref[2]
    return (((req << shift_of(groups)) | group) << shift_of(rows)) | (position & (rows - 1))


def pack(place, rows_ref, out_ref):
    width = rows_ref.shape[1]
    chunk = width // CUTS

    def cut(k, carry):
        part = pl.ds(pl.multiple_of(k * chunk, 128), chunk)
        out_ref[:, part] = jnp.dot(place, rows_ref[:, part], preferred_element_type=jnp.float32).astype(jnp.bfloat16)
        return carry

    lax.fori_loop(0, CUTS, cut, 0)


def route_kernel(sizes, top, pieces, where_ref, *refs):
    here = refs[:pieces]
    packed_ref, place_ref, table_ref, rows_ref = refs[pieces:]
    each, half = here[0].shape[0], here[0].shape[1] - TAIL
    experts, _, slots = table_ref.shape
    tokens = each * pieces
    for q in range(pieces):
        rows_ref[q * each : (q + 1) * each, :] = here[q][:, :half]
    tail = jnp.concatenate([ref[:, half:] for ref in here], axis=0).astype(jnp.float32)
    first = where_ref[1] * experts
    lane = lax.broadcasted_iota(jnp.int32, (tokens, TAIL), 1)
    gates = sum(pltpu.roll(tail, TAIL - top * part, 1) for part in (1, 2, 3))
    names = jnp.where(lane < top, tail, -1.0).astype(jnp.int32)
    present = jnp.zeros((tokens, TAIL), jnp.float32)
    weights = []
    for e in range(experts):
        named = names == first + e
        hit = jnp.sum(jnp.where(named, 1.0, 0.0), axis=1, keepdims=True)
        weights.append(jnp.sum(jnp.where(named, gates, 0.0), axis=1, keepdims=True))
        present = jnp.where(lane == e, hit, present)
    token = canonical(lax.broadcasted_iota(jnp.int32, (tokens, tokens), 0), where_ref, sizes)
    other = canonical(lax.broadcasted_iota(jnp.int32, (tokens, tokens), 1), where_ref, sizes)
    earlier = jnp.where(other < token, 1.0, 0.0).astype(jnp.bfloat16)
    rank = jnp.dot(earlier, present.astype(jnp.bfloat16), preferred_element_type=jnp.float32)
    rank = jnp.where(present > 0.0, rank, -1.0)
    token = canonical(lax.broadcasted_iota(jnp.int32, (tokens, 1), 0), where_ref, sizes).astype(jnp.float32)
    slot = lax.broadcasted_iota(jnp.int32, (tokens, slots), 1).astype(jnp.float32)
    for e in range(experts):
        column = jnp.sum(jnp.where(lane == e, rank, 0.0), axis=1, keepdims=True)
        used = slot == column
        table_ref[e, 0:1, :] = jnp.sum(jnp.where(used, weights[e], 0.0), axis=0, keepdims=True)
        table_ref[e, 1:2, :] = jnp.sum(jnp.where(used, token, 0.0), axis=0, keepdims=True)
        place_ref[e * slots : (e + 1) * slots, :] = jnp.where(used, 1.0, 0.0).T.astype(jnp.bfloat16)
    pack(place_ref[...], rows_ref, packed_ref)


def route(where, here, experts, sizes, top):
    pieces = len(here)
    each, half = here[0].shape[0], here[0].shape[1] - TAIL
    tokens = pieces * each
    slots = tokens // sizes[2] * CAP

    def kernel(*refs):
        route_kernel(sizes, top, pieces, *refs)

    nbytes = 2 * tokens * (half + 2 * TAIL) + 2 * experts * slots * (half // 2 + tokens) + 8 * tokens * (tokens + slots)
    return pl.pallas_call(
        kernel,
        out_shape=(
            jax.ShapeDtypeStruct((experts * slots, half), jnp.bfloat16),
            jax.ShapeDtypeStruct((experts * slots, tokens), jnp.bfloat16),
            jax.ShapeDtypeStruct((experts, 8, slots), jnp.float32),
        ),
        in_specs=[SMEM] + [VMEM] * pieces,
        out_specs=(VMEM, VMEM, VMEM),
        scratch_shapes=[pltpu.VMEM((tokens, half), jnp.bfloat16)],
        compiler_params=pltpu.CompilerParams(vmem_limit_bytes=2 * nbytes + 8 * MIB),
        cost_estimate=pl.CostEstimate(
            flops=2 * experts * slots * tokens * half, bytes_accessed=4 * experts * slots * half, transcendentals=0
        ),
        name="route",
    )(where, *here)


def in_order(copies):
    for copy in copies[:FLIGHT]:
        copy.start()

    def wait(index):
        copies[index].wait()
        if index + FLIGHT < len(copies):
            copies[index + FLIGHT].start()

    return wait


def hidden_units(where, place, packed, there, gate_held, up_weight):
    experts, features, units = up_weight.shape
    half = packed.shape[1]
    slots = packed.shape[0] // experts
    depth = min(RING, experts)
    pieces = len(there)
    tokens = place.shape[1]
    each = tokens // pieces

    def kernel(where_ref, place_ref, packed_ref, *refs):
        there_refs, refs = refs[:pieces], refs[pieces:]
        gate_refs, refs = refs[: len(gate_held)], refs[len(gate_held) :]
        up_ref, out_ref, ring_ref, rows_ref, other_ref, ring_sems, sems = refs
        gate_at = [(ref, e) for ref in gate_refs for e in range(ref.shape[0])]
        mine = pl.ds(pl.multiple_of(where_ref[0] * half, 128), half)
        others = pl.ds(pl.multiple_of((1 - where_ref[0]) * half, 128), half)
        wait = in_order([
            pltpu.make_async_copy(
                up_ref.at[e, rows, :], ring_ref.at[e % depth, rows, :], ring_sems.at[2 * (e % depth) + side]
            )
            for e in range(experts)
            for side, rows in enumerate((mine, others))
        ])
        copies = []
        for q in range(pieces):
            span = pl.ds(q * each, each)
            source = there_refs[q].at[:, pl.ds(0, half)]
            copies.append(pltpu.make_async_copy(source, rows_ref.at[span, :], sems.at[q]))
        for copy in copies:
            copy.start()
        for copy in copies:
            copy.wait()
        pack(place_ref[...], rows_ref, other_ref)
        for e in range(experts):
            span = slice(e * slots, (e + 1) * slots)
            gate_ref, index = gate_at[e]
            slot = e % depth
            gate_act = jnp.dot(packed_ref[span, :], gate_ref[index, mine, :], preferred_element_type=jnp.float32)
            gate_act += jnp.dot(other_ref[span, :], gate_ref[index, others, :], preferred_element_type=jnp.float32)
            wait(2 * e)
            up_act = jnp.dot(packed_ref[span, :], ring_ref[slot, mine, :], preferred_element_type=jnp.float32)
            wait(2 * e + 1)
            up_act += jnp.dot(other_ref[span, :], ring_ref[slot, others, :], preferred_element_type=jnp.float32)
            out_ref[e] = (gate_act / (1.0 + jnp.exp(-gate_act)) * up_act).astype(jnp.bfloat16)

    scratch = depth * features * units * 2 + tokens * half * 2 + experts * slots * half * 2
    work = 4 * experts * slots * half // CUTS + 24 * slots * units + 2 * slots * features
    return pl.pallas_call(
        kernel,
        out_shape=jax.ShapeDtypeStruct((experts, slots, units), jnp.bfloat16),
        in_specs=[SMEM, VMEM, VMEM] + [ANY] * pieces + [VMEM] * len(gate_held) + [HBM],
        out_specs=VMEM,
        scratch_shapes=[
            pltpu.VMEM((depth, features, units), jnp.bfloat16),
            pltpu.VMEM((tokens, half), jnp.bfloat16),
            pltpu.VMEM((experts * slots, half), jnp.bfloat16),
            pltpu.SemaphoreType.DMA((2 * depth,)),
            pltpu.SemaphoreType.DMA((pieces,)),
        ],
        compiler_params=pltpu.CompilerParams(vmem_limit_bytes=scratch + work + MIB),
        cost_estimate=pl.CostEstimate(
            flops=4 * experts * slots * features * units,
            bytes_accessed=2 * experts * features * units,
            transcendentals=experts * slots * units,
        ),
        name="gate_up",
    )(where, place, packed, *there, *map(in_vmem, gate_held), in_hbm(up_weight))


def down(where, table, here, there, down_held, tokens):
    reqs = lax.axis_size("req")
    experts, hidden, width = down_held.shape
    _, slots, part = here[0].shape
    pieces = len(here)
    share = tokens if reqs > 4 else tokens // reqs
    shapes = [jax.ShapeDtypeStruct((share, width), jnp.bfloat16)] * (tokens // share)

    def kernel(where_ref, table_ref, *refs):
        here_refs, there_refs, refs = refs[:pieces], refs[pieces : 2 * pieces], refs[2 * pieces :]
        down_ref, outs, (units_ref, acc_ref, sems) = refs[0], refs[1:-3], refs[-3:]
        copies = []
        for q in range(pieces):
            for side, source in ((0, here_refs[q]), (1, there_refs[q])):
                owner = (where_ref[0] ^ side) * pieces + (where_ref[2] ^ q)
                columns = pl.ds(pl.multiple_of(owner * part, 128), part)
                copies.append(pltpu.make_async_copy(source, units_ref.at[:, :, columns], sems.at[2 * q + side]))
        for copy in copies:
            copy.start()
        for copy in copies:
            copy.wait()
        token = lax.broadcasted_iota(jnp.int32, (tokens, slots), 0)
        for e in range(experts):
            projected = jnp.dot(units_ref[e], down_ref[e], preferred_element_type=jnp.float32).astype(jnp.bfloat16)
            named = token == table_ref[e, 1:2, :].astype(jnp.int32)
            weights = jnp.where(named, table_ref[e, 0:1, :], 0.0)
            upper = weights.astype(jnp.bfloat16)
            lower = (weights - upper.astype(jnp.float32)).astype(jnp.bfloat16)
            combined = jnp.dot(upper, projected, preferred_element_type=jnp.float32)
            combined += jnp.dot(lower, projected, preferred_element_type=jnp.float32)
            if e == 0:
                acc_ref[...] = combined
            else:
                acc_ref[...] += combined
        if len(outs) == 1:
            outs[0][...] = acc_ref[...].astype(jnp.bfloat16)
        else:
            for bits, out in enumerate(outs):
                start = pl.multiple_of((where_ref[1] ^ bits) * share, share)
                out[...] = acc_ref[pl.ds(start, share), :].astype(jnp.bfloat16)

    scratch = experts * slots * hidden * 2 + tokens * width * 4
    work = tokens * (slots * 16 + width * 12) + slots * width * 8
    return pl.pallas_call(
        kernel,
        out_shape=shapes,
        in_specs=[SMEM, VMEM] + [ANY] * (2 * pieces) + [VMEM],
        out_specs=[VMEM] * len(shapes),
        scratch_shapes=[
            pltpu.VMEM((experts, slots, hidden), jnp.bfloat16),
            pltpu.VMEM((tokens, width), jnp.float32),
            pltpu.SemaphoreType.DMA((2 * pieces,)),
        ],
        compiler_params=pltpu.CompilerParams(vmem_limit_bytes=scratch + work + 2 * MIB),
        cost_estimate=pl.CostEstimate(
            flops=2 * experts * slots * hidden * width,
            bytes_accessed=2 * experts * hidden * width,
            transcendentals=0,
        ),
        name="down",
    )(where, table, *here, *there, in_vmem(down_held))


def sum_over_req(where, parts, groups, rows):
    width = parts[0].shape[-1]

    def kernel(where_ref, *refs):
        inputs, outs, acc_ref = refs[: len(parts)], refs[len(parts) : -1], refs[-1]
        total = None
        for part in inputs:
            for block in range(part.shape[0]):
                value = part[block].astype(jnp.float32)
                total = value if total is None else total + value
        acc_ref[...] = total
        for bits, out in enumerate(outs):
            start = pl.multiple_of((where_ref[2] ^ bits) * rows, rows)
            out[...] = acc_ref[pl.ds(start, rows), :].astype(jnp.bfloat16)

    return pl.pallas_call(
        kernel,
        out_shape=[jax.ShapeDtypeStruct((rows, width), jnp.bfloat16)] * groups,
        in_specs=[SMEM] + [VMEM] * len(parts),
        out_specs=[VMEM] * groups,
        scratch_shapes=[pltpu.VMEM((groups * rows, width), jnp.float32)],
        compiler_params=pltpu.CompilerParams(vmem_limit_bytes=8 * MIB),
        name="sum_req",
    )(where, *parts)


def mix(where, hidden, parts):
    def kernel(where_ref, hidden_ref, *refs):
        out_ref = refs[-1]
        for bits, part in enumerate(refs[:-1]):
            width = part.shape[1]
            columns = pl.ds(pl.multiple_of((where_ref[2] ^ bits) * width, 128), width)
            out_ref[:, columns] = (hidden_ref[:, columns] + part[...].astype(jnp.float32)).astype(jnp.bfloat16)

    return pl.pallas_call(
        kernel,
        out_shape=jax.ShapeDtypeStruct(hidden.shape, jnp.bfloat16),
        in_specs=[SMEM, VMEM] + [VMEM] * len(parts),
        out_specs=VMEM,
        compiler_params=pltpu.CompilerParams(vmem_limit_bytes=4 * MIB),
        name="mix",
    )(where, hidden, *parts)


def on_device(residual, attn_part, norm_gain, routes, gates, gate_weight, up_weight, down_weight):
    reqs, groups = lax.axis_size("req"), lax.axis_size("grp")
    rows, top = routes.shape
    tokens = reqs * groups * rows
    spots = [lax.axis_index(axis) for axis in ("head", "req", "grp")]
    where = jnp.stack(spots).astype(jnp.int32)
    experts = gate_weight.shape[0]
    attn = attn_part[0]
    there = [swap(attn, "head", 1), swap(residual, "head", 1)]
    base, tail, gain = prepare(where, attn, residual, routes, gates, norm_gain[None, :])
    there, base, tail, gain = lax.optimization_barrier((there, base, tail, gain))
    hidden, packet = norm(where, base, there[0], there[1], gain, tail)

    early = experts * 3 // 8
    first = stage([(gate_weight, 0, early)], packet)
    column, first = gather_rows(packet, "req", first)
    second = stage([(gate_weight, early, experts)], column)
    here = [column] + [swap(column, "grp", bits) for bits in range(1, groups)]
    here, second = lax.optimization_barrier((here, second))
    there = [swap(piece, "head", 1) for piece in here]
    packed, place, table = route(where, here, experts, (reqs, groups, rows), top)
    units = hidden_units(where, place, packed, there, first + second, up_weight)

    held = stage([(down_weight, 0, experts)], units)
    here = [units] + [swap(units, "grp", bits) for bits in range(1, groups)]
    here, held = lax.optimization_barrier((here, held))
    there = [swap(piece, "head", 1) for piece in here]
    partial = down(where, table, here, there, held[0], tokens)

    if reqs > 4:
        parts = partial[0].reshape(reqs, groups * rows, -1)
        parts = [lax.all_to_all(parts, "req", split_axis=0, concat_axis=0, tiled=True)]
    else:
        parts = [partial[0]] + [swap(partial[bits], "req", bits) for bits in range(1, reqs)]
        parts = [part[None] for part in parts]
    sums = sum_over_req(where, parts, groups, rows)
    sums = [sums[0]] + [swap(sums[bits], "grp", bits) for bits in range(1, groups)]
    return mix(where, hidden, sums)


def solution(mesh):
    placed = (
        P(("req", "grp"), "head"),
        P("head", ("req", "grp"), None),
        P("head"),
        P(("req", "grp"), None),
        P(("req", "grp"), None),
        P("req", None, ("head", "grp")),
        P("req", None, ("head", "grp")),
        P("req", None, ("head", "grp")),
    )
    return jax.shard_map(
        on_device, mesh=mesh, in_specs=placed, out_specs=P(("req", "grp"), "head"), check_vma=False
    )
```

```python
import jax
import jax.numpy as jnp
from jax import lax
from jax.experimental import pallas as pl
from jax.experimental.pallas import tpu as pltpu
from jax.sharding import PartitionSpec as P

CAP = 4
EPSILON = 1e-06
TAIL = 128
CUTS = 4
AHEAD = 2
RING = 3
MIB = 1024 * 1024
VMEM = pl.BlockSpec(memory_space=pltpu.VMEM)
SMEM = pl.BlockSpec(memory_space=pltpu.SMEM)
ANY = pl.BlockSpec(memory_space=pl.ANY)
HBM = pl.BlockSpec(memory_space=pltpu.HBM)


def swap(array, axis, bits):
    return lax.ppermute(array, axis, [(i, i ^ bits) for i in range(lax.axis_size(axis))])


def gather_rows(array, axis, meanwhile):
    count = lax.axis_size(axis)
    if count > 4:
        return lax.all_gather(array, axis, axis=0, tiled=True), meanwhile
    pieces = [array] + [swap(array, axis, bits) for bits in range(1, count)]
    pieces, meanwhile = lax.optimization_barrier((pieces, meanwhile))

    def kernel(*refs):
        refs[-1][...] = jnp.concatenate([ref[...] for ref in refs[:-1]], axis=0)

    rows = pl.pallas_call(
        kernel,
        out_shape=jax.ShapeDtypeStruct((count * array.shape[0], array.shape[1]), array.dtype),
        in_specs=[VMEM] * count,
        out_specs=VMEM,
        compiler_params=pltpu.CompilerParams(vmem_limit_bytes=4 * MIB),
        name="collect",
    )(*pieces)
    return rows, meanwhile


def prepare_kernel(where_ref, *refs):
    sources, (base_ref, tail_ref, out_gain_ref), refs = refs[:5], refs[5:8], refs[8:]
    copies_to, wide_ref, sems = refs[:4], refs[4], refs[5]
    copies = [
        pltpu.make_async_copy(source, target, sems.at[index])
        for index, (source, target) in enumerate(zip(sources, (*copies_to, out_gain_ref)))
    ]
    for copy in copies:
        copy.start()
    for copy in copies:
        copy.wait()
    attn_ref, res_ref, routes_ref, gates_ref = copies_to
    half = res_ref.shape[1]
    top = routes_ref.shape[1]
    here = pl.ds(pl.multiple_of(where_ref[0] * half, 128), half)
    base_ref[...] = attn_ref[...].astype(jnp.float32)
    base_ref[:, here] += res_ref[...].astype(jnp.float32)
    gates = gates_ref[...]
    upper = gates.astype(jnp.bfloat16).astype(jnp.float32)
    middle = (gates - upper).astype(jnp.bfloat16).astype(jnp.float32)
    wide_ref[...] = jnp.zeros_like(wide_ref)
    for index, part in enumerate((routes_ref[...].astype(jnp.float32), upper, middle, gates - upper - middle)):
        wide_ref[:, index * top : (index + 1) * top] = part
    tail_ref[...] = wide_ref[...].astype(jnp.bfloat16)


def prepare(where, attn, residual, routes, gates, gain):
    rows = residual.shape[0]
    arrays = [attn, residual, routes, gates]
    return pl.pallas_call(
        prepare_kernel,
        out_shape=(
            jax.ShapeDtypeStruct(attn.shape, jnp.float32),
            jax.ShapeDtypeStruct((rows, TAIL), jnp.bfloat16),
            jax.ShapeDtypeStruct(gain.shape, jnp.float32),
        ),
        in_specs=[SMEM] + [HBM] * 5,
        out_specs=(VMEM, VMEM, VMEM),
        scratch_shapes=[pltpu.VMEM(array.shape, array.dtype) for array in arrays]
        + [pltpu.VMEM((rows, TAIL), jnp.float32), pltpu.SemaphoreType.DMA((5,))],
        compiler_params=pltpu.CompilerParams(vmem_limit_bytes=4 * MIB),
        name="prepare",
    )(where, *[in_hbm(array) for array in (*arrays, gain)])


def norm_kernel(where_ref, base_ref, attn_there_ref, res_there_ref, gain_ref, tail_ref, hidden_ref, packet_ref):
    half = res_there_ref.shape[1]
    here = pl.ds(pl.multiple_of(where_ref[0] * half, 128), half)
    there = pl.ds(pl.multiple_of((1 - where_ref[0]) * half, 128), half)
    hidden = base_ref[:, here] + attn_there_ref[:, here].astype(jnp.float32)
    other = base_ref[:, there] + attn_there_ref[:, there].astype(jnp.float32) + res_there_ref[...].astype(jnp.float32)
    squares = jnp.sum(hidden * hidden, axis=1, keepdims=True) + jnp.sum(other * other, axis=1, keepdims=True)
    row_scale = lax.rsqrt(squares / (2 * half) + EPSILON)
    hidden_ref[...] = hidden
    packet_ref[:, :half] = (hidden * row_scale * gain_ref[...][None, :]).astype(jnp.bfloat16)
    packet_ref[:, half:] = tail_ref[...]


def norm(where, base, attn_there, residual_there, gain, tail):
    rows, half = residual_there.shape
    return pl.pallas_call(
        norm_kernel,
        out_shape=(
            jax.ShapeDtypeStruct((rows, half), jnp.float32),
            jax.ShapeDtypeStruct((rows, half + TAIL), jnp.bfloat16),
        ),
        in_specs=[SMEM] + [VMEM] * 5,
        out_specs=(VMEM, VMEM),
        compiler_params=pltpu.CompilerParams(vmem_limit_bytes=4 * MIB),
        name="norm",
    )(where, base, attn_there, residual_there, gain, tail)


def in_hbm(array):
    return pltpu.with_memory_space_constraint(array, pltpu.HBM)


def in_vmem(array):
    return pltpu.with_memory_space_constraint(array, pltpu.VMEM)


def stage(weights, after=None):
    weights = [(array, first, end) for array, first, end in weights if end > first]
    if not weights:
        return []
    spans = [(first, end) for _, first, end in weights]
    extra = [] if after is None else [after]

    def kernel(*refs):
        inputs, outs, sems = refs[: len(spans)], refs[len(spans) + len(extra) : -1], refs[-1]
        copies = []
        for source, target, (first, end) in zip(inputs, outs, spans):
            for e in range(end - first):
                copies.append(pltpu.make_async_copy(source.at[first + e], target.at[e], sems.at[len(copies)]))
        for copy in copies:
            copy.start()
        for copy in copies:
            copy.wait()

    count = sum(end - first for first, end in spans)
    nbytes = sum((end - first) * array[0].size * 2 for array, first, end in weights)
    copies = pl.pallas_call(
        kernel,
        out_shape=[pltpu.VMEM((end - first, *array.shape[1:]), array.dtype) for array, first, end in weights],
        in_specs=[HBM] * len(spans) + [ANY] * len(extra),
        out_specs=[VMEM] * len(spans),
        scratch_shapes=[pltpu.SemaphoreType.DMA((count,))],
        compiler_params=pltpu.CompilerParams(vmem_limit_bytes=MIB),
        cost_estimate=pl.CostEstimate(flops=0, bytes_accessed=nbytes, transcendentals=0),
        name="stage",
    )(*[in_hbm(array) for array, _, _ in weights], *extra)
    return list(copies)


def shift_of(count):
    return count.bit_length() - 1


def canonical(position, where_ref, sizes):
    reqs, groups, rows = sizes
    req = (position >> shift_of(rows)) & (reqs - 1)
    if reqs <= 4:
        req = req ^ where_ref[1]
    group = (position >> shift_of(rows * reqs)) ^ where_ref[2]
    return (((req << shift_of(groups)) | group) << shift_of(rows)) | (position & (rows - 1))


def pack(place, rows_ref, out_ref):
    width = rows_ref.shape[1]
    chunk = width // CUTS

    def cut(k, carry):
        part = pl.ds(pl.multiple_of(k * chunk, 128), chunk)
        out_ref[:, part] = jnp.dot(place, rows_ref[:, part], preferred_element_type=jnp.float32).astype(jnp.bfloat16)
        return carry

    lax.fori_loop(0, CUTS, cut, 0)


def route_kernel(sizes, top, pieces, where_ref, *refs):
    here = refs[:pieces]
    packed_ref, place_ref, table_ref, count_ref, rows_ref = refs[pieces:]
    each, half = here[0].shape[0], here[0].shape[1] - TAIL
    experts, _, slots = table_ref.shape
    tokens = each * pieces
    for q in range(pieces):
        rows_ref[q * each : (q + 1) * each, :] = here[q][:, :half]
    tail = jnp.concatenate([ref[:, half:] for ref in here], axis=0).astype(jnp.float32)
    first = where_ref[1] * experts
    lane = lax.broadcasted_iota(jnp.int32, (tokens, TAIL), 1)
    gates = sum(pltpu.roll(tail, TAIL - top * part, 1) for part in (1, 2, 3))
    names = jnp.where(lane < top, tail, -1.0).astype(jnp.int32)
    present = jnp.zeros((tokens, TAIL), jnp.float32)
    weights = []
    for e in range(experts):
        named = names == first + e
        hit = jnp.sum(jnp.where(named, 1.0, 0.0), axis=1, keepdims=True)
        weights.append(jnp.sum(jnp.where(named, gates, 0.0), axis=1, keepdims=True))
        present = jnp.where(lane == e, hit, present)
    token = canonical(lax.broadcasted_iota(jnp.int32, (tokens, tokens), 0), where_ref, sizes)
    other = canonical(lax.broadcasted_iota(jnp.int32, (tokens, tokens), 1), where_ref, sizes)
    earlier = jnp.where(other < token, 1.0, 0.0).astype(jnp.bfloat16)
    rank = jnp.dot(earlier, present.astype(jnp.bfloat16), preferred_element_type=jnp.float32)
    rank = jnp.where(present > 0.0, rank, -1.0)
    token = canonical(lax.broadcasted_iota(jnp.int32, (tokens, 1), 0), where_ref, sizes).astype(jnp.float32)
    slot = lax.broadcasted_iota(jnp.int32, (tokens, slots), 1).astype(jnp.float32)
    for e in range(experts):
        column = jnp.sum(jnp.where(lane == e, rank, 0.0), axis=1, keepdims=True)
        used = slot == column
        table_ref[e, 0:1, :] = jnp.sum(jnp.where(used, weights[e], 0.0), axis=0, keepdims=True)
        table_ref[e, 1:2, :] = jnp.sum(jnp.where(used, token, 0.0), axis=0, keepdims=True)
        place_ref[e * slots : (e + 1) * slots, :] = jnp.where(used, 1.0, 0.0).T.astype(jnp.bfloat16)
        count_ref[e] = jnp.sum(jnp.where(lane == e, present, 0.0)).astype(jnp.int32)
    pack(place_ref[...], rows_ref, packed_ref)


def route(where, here, experts, sizes, top):
    pieces = len(here)
    each, half = here[0].shape[0], here[0].shape[1] - TAIL
    tokens = pieces * each
    slots = tokens // sizes[2] * CAP

    def kernel(*refs):
        route_kernel(sizes, top, pieces, *refs)

    nbytes = 2 * tokens * (half + 2 * TAIL) + 2 * experts * slots * (half // 2 + tokens) + 8 * tokens * (tokens + slots)
    return pl.pallas_call(
        kernel,
        out_shape=(
            jax.ShapeDtypeStruct((experts * slots, half), jnp.bfloat16),
            jax.ShapeDtypeStruct((experts * slots, tokens), jnp.bfloat16),
            jax.ShapeDtypeStruct((experts, 8, slots), jnp.float32),
            jax.ShapeDtypeStruct((experts,), jnp.int32),
        ),
        in_specs=[SMEM] + [VMEM] * pieces,
        out_specs=(VMEM, VMEM, VMEM, SMEM),
        scratch_shapes=[pltpu.VMEM((tokens, half), jnp.bfloat16)],
        compiler_params=pltpu.CompilerParams(vmem_limit_bytes=2 * nbytes + 8 * MIB),
        cost_estimate=pl.CostEstimate(
            flops=2 * experts * slots * tokens * half, bytes_accessed=4 * experts * slots * half, transcendentals=0
        ),
        name="route",
    )(where, *here)


def per_count(count, slots, run):
    last = -1
    for rows in (slots // 2, slots * 3 // 4, slots):

        @pl.when((count > last) & (count <= rows))
        def _(rows=rows):
            run(rows)

        last = rows


def hidden_units(where, count, place, packed, there, gate_held, up_weight):
    experts, features, units = up_weight.shape
    half = packed.shape[1]
    slots = packed.shape[0] // experts
    depth = min(RING, experts)
    pieces = len(there)
    tokens = place.shape[1]
    each = tokens // pieces

    def kernel(where_ref, count_ref, place_ref, packed_ref, *refs):
        there_refs, refs = refs[:pieces], refs[pieces:]
        gate_refs, refs = refs[: len(gate_held)], refs[len(gate_held) :]
        up_ref, out_ref, ring_ref, rows_ref, other_ref, ring_sems, sems = refs
        mine = pl.ds(pl.multiple_of(where_ref[0] * half, 128), half)
        others = pl.ds(pl.multiple_of((1 - where_ref[0]) * half, 128), half)

        def load(e, side):
            rows = (mine, others)[side]
            slot = lax.rem(e, depth)
            return pltpu.make_async_copy(
                up_ref.at[e, rows, :], ring_ref.at[slot, rows, :], ring_sems.at[2 * slot + side]
            )

        for e in range(min(AHEAD, experts)):
            load(e, 0).start()
            load(e, 1).start()
        copies = []
        for q in range(pieces):
            span = pl.ds(q * each, each)
            source = there_refs[q].at[:, pl.ds(0, half)]
            copies.append(pltpu.make_async_copy(source, rows_ref.at[span, :], sems.at[q]))
        for copy in copies:
            copy.start()
        for copy in copies:
            copy.wait()
        pack(place_ref[...], rows_ref, other_ref)
        def expert(e, gate_ref, index):
            slot = lax.rem(e, depth)
            for side in (0, 1):
                load(e, side).wait()

                @pl.when(e + AHEAD < experts)
                def _(side=side):
                    load(e + AHEAD, side).start()

            def run(rows):
                span = pl.ds(pl.multiple_of(e * slots, slots), rows)

                def project(weight, at):
                    here = jnp.dot(packed_ref[span, :], weight[at, mine, :], preferred_element_type=jnp.float32)
                    return here + jnp.dot(other_ref[span, :], weight[at, others, :], preferred_element_type=jnp.float32)

                gate_act = project(gate_ref, index)
                up_act = project(ring_ref, slot)
                units_now = gate_act / (1.0 + jnp.exp(-gate_act)) * up_act
                out_ref[e, 0:rows, :] = units_now.astype(jnp.bfloat16)
                if rows < slots:
                    out_ref[e, rows:slots, :] = jnp.zeros((slots - rows, units), jnp.bfloat16)

            per_count(count_ref[e], slots, run)

        done = 0
        for gate_ref in gate_refs:

            def step(index, carry, done=done, gate_ref=gate_ref):
                expert(done + index, gate_ref, index)
                return carry

            lax.fori_loop(0, gate_ref.shape[0], step, 0)
            done += gate_ref.shape[0]

    scratch = depth * features * units * 2 + tokens * half * 2 + experts * slots * half * 2
    work = 4 * experts * slots * half // CUTS + 24 * slots * units + 2 * slots * features
    return pl.pallas_call(
        kernel,
        out_shape=jax.ShapeDtypeStruct((experts, slots, units), jnp.bfloat16),
        in_specs=[SMEM, SMEM, VMEM, VMEM] + [ANY] * pieces + [VMEM] * len(gate_held) + [HBM],
        out_specs=VMEM,
        scratch_shapes=[
            pltpu.VMEM((depth, features, units), jnp.bfloat16),
            pltpu.VMEM((tokens, half), jnp.bfloat16),
            pltpu.VMEM((experts * slots, half), jnp.bfloat16),
            pltpu.SemaphoreType.DMA((2 * depth,)),
            pltpu.SemaphoreType.DMA((pieces,)),
        ],
        compiler_params=pltpu.CompilerParams(vmem_limit_bytes=scratch + work + MIB),
        cost_estimate=pl.CostEstimate(
            flops=4 * experts * slots * features * units,
            bytes_accessed=2 * experts * features * units,
            transcendentals=experts * slots * units,
        ),
        name="gate_up",
    )(where, count, place, packed, *there, *map(in_vmem, gate_held), in_hbm(up_weight))


def down(where, table, here, there, down_held, tokens):
    reqs = lax.axis_size("req")
    experts, hidden, width = down_held.shape
    _, slots, part = here[0].shape
    pieces = len(here)
    share = tokens if reqs > 4 else tokens // reqs
    shapes = [jax.ShapeDtypeStruct((share, width), jnp.bfloat16)] * (tokens // share)

    def kernel(where_ref, table_ref, *refs):
        here_refs, there_refs, refs = refs[:pieces], refs[pieces : 2 * pieces], refs[2 * pieces :]
        down_ref, outs, (units_ref, acc_ref, sems) = refs[0], refs[1:-3], refs[-3:]
        copies = []
        for e in range(experts):
            for q in range(pieces):
                for side, source in ((0, here_refs[q]), (1, there_refs[q])):
                    owner = (where_ref[0] ^ side) * pieces + (where_ref[2] ^ q)
                    columns = pl.ds(pl.multiple_of(owner * part, 128), part)
                    target = units_ref.at[e, :, columns]
                    copies.append(pltpu.make_async_copy(source.at[e], target, sems.at[len(copies)]))
        for copy in copies:
            copy.start()
        token = lax.broadcasted_iota(jnp.int32, (tokens, slots), 0)
        for e in range(experts):
            for copy in copies[e * 2 * pieces : (e + 1) * 2 * pieces]:
                copy.wait()
            projected = jnp.dot(units_ref[e], down_ref[e], preferred_element_type=jnp.float32).astype(jnp.bfloat16)
            named = token == table_ref[e, 1:2, :].astype(jnp.int32)
            weights = jnp.where(named, table_ref[e, 0:1, :], 0.0)
            upper = weights.astype(jnp.bfloat16)
            lower = (weights - upper.astype(jnp.float32)).astype(jnp.bfloat16)
            combined = jnp.dot(upper, projected, preferred_element_type=jnp.float32)
            combined += jnp.dot(lower, projected, preferred_element_type=jnp.float32)
            if e == 0:
                acc_ref[...] = combined
            else:
                acc_ref[...] += combined
        if len(outs) == 1:
            outs[0][...] = acc_ref[...].astype(jnp.bfloat16)
        else:
            for bits, out in enumerate(outs):
                start = pl.multiple_of((where_ref[1] ^ bits) * share, share)
                out[...] = acc_ref[pl.ds(start, share), :].astype(jnp.bfloat16)

    scratch = experts * slots * hidden * 2 + tokens * width * 4
    work = tokens * (slots * 16 + width * 12) + slots * width * 8
    return pl.pallas_call(
        kernel,
        out_shape=shapes,
        in_specs=[SMEM, VMEM] + [ANY] * (2 * pieces) + [VMEM],
        out_specs=[VMEM] * len(shapes),
        scratch_shapes=[
            pltpu.VMEM((experts, slots, hidden), jnp.bfloat16),
            pltpu.VMEM((tokens, width), jnp.float32),
            pltpu.SemaphoreType.DMA((experts * 2 * pieces,)),
        ],
        compiler_params=pltpu.CompilerParams(vmem_limit_bytes=scratch + work + 4 * MIB),
        cost_estimate=pl.CostEstimate(
            flops=2 * experts * slots * hidden * width,
            bytes_accessed=2 * experts * hidden * width,
            transcendentals=0,
        ),
        name="down",
    )(where, table, *here, *there, in_vmem(down_held))


def sum_over_req(where, parts, groups, rows):
    width = parts[0].shape[-1]

    def kernel(where_ref, *refs):
        inputs, outs, acc_ref = refs[: len(parts)], refs[len(parts) : -1], refs[-1]
        total = None
        for part in inputs:
            for block in range(part.shape[0]):
                value = part[block].astype(jnp.float32)
                total = value if total is None else total + value
        acc_ref[...] = total
        for bits, out in enumerate(outs):
            start = pl.multiple_of((where_ref[2] ^ bits) * rows, rows)
            out[...] = acc_ref[pl.ds(start, rows), :].astype(jnp.bfloat16)

    return pl.pallas_call(
        kernel,
        out_shape=[jax.ShapeDtypeStruct((rows, width), jnp.bfloat16)] * groups,
        in_specs=[SMEM] + [VMEM] * len(parts),
        out_specs=[VMEM] * groups,
        scratch_shapes=[pltpu.VMEM((groups * rows, width), jnp.float32)],
        compiler_params=pltpu.CompilerParams(vmem_limit_bytes=8 * MIB),
        name="sum_req",
    )(where, *parts)


def mix(where, hidden, parts):
    def kernel(where_ref, hidden_ref, *refs):
        out_ref = refs[-1]
        for bits, part in enumerate(refs[:-1]):
            width = part.shape[1]
            columns = pl.ds(pl.multiple_of((where_ref[2] ^ bits) * width, 128), width)
            out_ref[:, columns] = (hidden_ref[:, columns] + part[...].astype(jnp.float32)).astype(jnp.bfloat16)

    return pl.pallas_call(
        kernel,
        out_shape=jax.ShapeDtypeStruct(hidden.shape, jnp.bfloat16),
        in_specs=[SMEM, VMEM] + [VMEM] * len(parts),
        out_specs=VMEM,
        compiler_params=pltpu.CompilerParams(vmem_limit_bytes=4 * MIB),
        name="mix",
    )(where, hidden, *parts)


def on_device(residual, attn_part, norm_gain, routes, gates, gate_weight, up_weight, down_weight):
    reqs, groups = lax.axis_size("req"), lax.axis_size("grp")
    rows, top = routes.shape
    tokens = reqs * groups * rows
    spots = [lax.axis_index(axis) for axis in ("head", "req", "grp")]
    where = jnp.stack(spots).astype(jnp.int32)
    experts = gate_weight.shape[0]
    attn = attn_part[0]
    there = [swap(attn, "head", 1), swap(residual, "head", 1)]
    base, tail, gain = prepare(where, attn, residual, routes, gates, norm_gain)
    there, base, tail, gain = lax.optimization_barrier((there, base, tail, gain))
    hidden, packet = norm(where, base, there[0], there[1], gain, tail)

    early = experts * 3 // 8
    first = stage([(gate_weight, 0, early)], packet)
    column, first = gather_rows(packet, "req", first)
    here = [column] + [swap(column, "grp", bits) for bits in range(1, groups)]
    there = [swap(column, "head", 1)]
    second = stage([(gate_weight, early, experts)], there[0])
    here[1:], second = lax.optimization_barrier((here[1:], second))
    there += [swap(piece, "head", 1) for piece in here[1:]]
    packed, place, table, count = route(where, here, experts, (reqs, groups, rows), top)
    units = hidden_units(where, count, place, packed, there, first + second, up_weight)

    held = stage([(down_weight, 0, experts)], units)
    here = [units] + [swap(units, "grp", bits) for bits in range(1, groups)]
    there = [swap(units, "head", 1)]
    here[1:], held = lax.optimization_barrier((here[1:], held))
    there += [swap(piece, "head", 1) for piece in here[1:]]
    partial = down(where, table, here, there, held[0], tokens)

    if reqs > 4:
        parts = partial[0].reshape(reqs, groups * rows, -1)
        parts = [lax.all_to_all(parts, "req", split_axis=0, concat_axis=0, tiled=True)]
    else:
        parts = [partial[0]] + [swap(partial[bits], "req", bits) for bits in range(1, reqs)]
        parts = [part[None] for part in parts]
    sums = sum_over_req(where, parts, groups, rows)
    sums = [sums[0]] + [swap(sums[bits], "grp", bits) for bits in range(1, groups)]
    return mix(where, hidden, sums)


def solution(mesh):
    placed = (
        P(("req", "grp"), "head"),
        P("head", ("req", "grp"), None),
        P("head"),
        P(("req", "grp"), None),
        P(("req", "grp"), None),
        P("req", None, ("head", "grp")),
        P("req", None, ("head", "grp")),
        P("req", None, ("head", "grp")),
    )
    return jax.shard_map(
        on_device, mesh=mesh, in_specs=placed, out_specs=P(("req", "grp"), "head"), check_vma=False
    )
```
